32 devices in a mesh: replica: 2 (over x), fsdp: 16 (over z, y, core).
Axes of the slice: x: 2, y: 2, z: 4, core: 2. Of those that a mesh axis runs over, the one named last changes fastest.
Arguments:
- master: float32 [2, 8192, 512], P('replica', 'fsdp'), may hold values from -0.0625 to 0.0625
- momentum: float32 [2, 8192, 512], P('replica', 'fsdp'), may hold values from -0.03125 to 0.03125
- working: bfloat16 [2, 8192, 512], P('replica', 'fsdp'), may hold values from -0.0625 to 0.0625
- tokens: bfloat16 [2, 3072, 8192], P('replica', 'fsdp'), may hold values from -6 to 6
- partners: int32 [2, 4], replicated, may hold values from 0 to 1, as said below
- mix_weights: int32 [2, 5], replicated, may hold values from 1 to 3
Outputs:
- new_master: float32 [2, 8192, 512], P('replica', 'fsdp')
- new_momentum: float32 [2, 8192, 512], P('replica', 'fsdp')
- keys: bfloat16 [2, 3072, 512], P('replica', 'fsdp')
The draws below stay inside these ranges and needn't reach their ends.
Inputs may be any that keep to these rules, and one draw needn't show every extreme that they name: partners[g, 0] is a perfect matching of the groups (never g itself, and symmetric); partners[g, 1..3] are any groups, g itself included, repeats allowed.
All inputs are finite; a program needn't handle non-finite values.
Results may differ from the reference program's by a relative error of at most 0.0049.
Values may be sent and summed in bfloat16 or wider, within the bound.
No kernel may reach another device: no remote copies, remote signals or barrier semaphores. Data moves between devices by JAX's collectives and lax.ppermute only.
A program may use at most 64 MiB of HBM per device.

```python
import jax
import jax.numpy as jnp
from jax import lax

D = 8192
KW = 512
TOKENS = 3072
GROUPS = 2


def draw_partners(key, part):
    key = jax.random.fold_in(key, 3)
    first_key = jax.random.fold_in(key, 11)
    extra_key = jax.random.fold_in(key, 12)
    order = jax.random.permutation(first_key, GROUPS).astype(jnp.int32)
    first = jnp.zeros((GROUPS,), jnp.int32)
    first = first.at[order[0::2]].set(order[1::2]).at[order[1::2]].set(order[0::2])
    extra = jax.random.randint(extra_key, (GROUPS, 3), 0, GROUPS).astype(jnp.int32)
    return jnp.concatenate([first[:, None], extra], axis=1).astype(jnp.int32)


def draw_mix_weights(key, part):
    key = jax.random.fold_in(key, 5)
    numerators = jax.random.randint(key, (GROUPS, 5), 1, 4).astype(jnp.int32)
    numerators = numerators.at[0, 0].set(3).at[0, 1].set(1)
    return numerators.astype(jnp.int32)


def level_of(key, shape, cuts, least, high):
    level = 1.0
    for axis_at, shards_of in cuts:
        draws = jax.random.uniform(jax.random.fold_in(jax.random.fold_in(key, 6), axis_at), (shards_of,), jnp.float32, least / len(cuts), high / len(cuts))
        level = level * jnp.repeat(jnp.exp(draws), shape[axis_at] // shards_of).reshape((-1,) + (1,) * (len(shape) - 1 - axis_at))
    return level


def centred(stream_key, dims, spread, bound, split=(), held_as=jnp.bfloat16):
    values = spread * jax.random.normal(stream_key, dims, jnp.float32)
    if split:
        values = values * level_of(stream_key, dims, split, -0.22, 0.18)
    return jnp.clip(values, -bound, bound).astype(held_as)


def setup_inputs(seed: int = 0) -> dict:
    seeds = jax.random.split(jax.random.key(seed), 7)
    master = centred(seeds[0], (GROUPS, D, KW), D ** -0.5, 0.0625, ((0, 2), (1, 16)), jnp.float32)
    momentum = centred(seeds[1], (GROUPS, D, KW), (4 * D) ** -0.5, 0.03125, ((0, 2), (1, 16)), jnp.float32)
    working = centred(seeds[2], (GROUPS, D, KW), D ** -0.5, 0.0625, ((0, 2), (1, 16)))
    tokens = centred(seeds[3], (GROUPS, TOKENS, D), 1.0, 6.0, ((0, 2), (1, 16)))
    partners = draw_partners(jax.random.fold_in(seeds[6], 71), 0)
    mix_weights = draw_mix_weights(jax.random.fold_in(seeds[6], 71), 0)
    return {"master": master, "momentum": momentum, "working": working, "tokens": tokens, "partners": partners, "mix_weights": mix_weights}


outer_rate = 0.7
momentum_decay = 0.9


def reference(master, momentum, working, tokens, partners, mix_weights):
    delta = master - working.astype(jnp.float32)
    group_ids = jnp.arange(GROUPS, dtype=jnp.int32)
    weights_f = mix_weights.astype(jnp.float32)
    mixing = weights_f[:, 0:1] * (group_ids[None, :] == group_ids[:, None]).astype(jnp.float32)
    for slot in range(4):
        mixing = mixing + weights_f[:, slot + 1:slot + 2] * (group_ids[None, :] == partners[:, slot:slot + 1]).astype(jnp.float32)
    total = jnp.sum(weights_f, axis=1)
    mixed = jnp.einsum("gh,hrk->grk", mixing, delta, precision=lax.Precision.HIGHEST) / total[:, None, None]
    new_momentum = momentum_decay * momentum + mixed
    new_master = master - outer_rate * (mixed + momentum_decay * new_momentum)
    fresh = new_master.astype(jnp.bfloat16)

    def group_keys(pair):
        inputs, weight = pair
        return jnp.dot(inputs, weight, preferred_element_type=jnp.float32).astype(jnp.bfloat16)

    keys = lax.map(group_keys, (tokens, fresh))
    return new_master, new_momentum, keys
```

```python
import jax
import jax.numpy as jnp
from jax import lax
from jax.experimental import pallas as pl
from jax.experimental.pallas import tpu as pltpu
from jax.sharding import PartitionSpec as P

outer_rate = 0.7
momentum_decay = 0.9
PLANE = 4
CHUNKS = 2


def plane_pairs(size, bit):
    return [(i, i ^ bit) for i in range(size)]


def line_pairs(size, to):
    return [(i, to[i // PLANE] * PLANE + i % PLANE) for i in range(size)]


def arrange_body(order, *refs):
    for source, target in zip(refs[:PLANE], refs[PLANE:]):
        target[...] = source[...]


def arrange_tokens(tokens, order, width):
    rows, blocks = tokens.shape[0], order.shape[0] // PLANE

    def column(distance):
        return lambda k, order: (0, order[k * PLANE + distance])

    return pl.pallas_call(
        arrange_body,
        grid_spec=pltpu.PrefetchScalarGridSpec(
            num_scalar_prefetch=1,
            grid=(blocks,),
            in_specs=[pl.BlockSpec((rows, width), column(d)) for d in range(PLANE)],
            out_specs=[pl.BlockSpec((rows, width), lambda k, order: (0, k))] * PLANE,
        ),
        out_shape=[jax.ShapeDtypeStruct((rows, blocks * width), tokens.dtype)] * PLANE,
        name="arrange_tokens",
    )(order, *([tokens] * PLANE))


def product(tokens, weights):
    return jnp.dot(tokens, weights, preferred_element_type=jnp.float32)


def shards(master, momentum, working, tokens, partners, mix_weights):
    groups = lax.axis_size("replica")
    size = lax.axis_size("fsdp")
    line = size // PLANE
    own_group = lax.axis_index("replica")
    place = lax.axis_index("fsdp")
    master, momentum, working, tokens = master[0], momentum[0], working[0], tokens[0]
    rows = master.shape[0]
    chunks = CHUNKS if rows % (CHUNKS * 16) == 0 else 1
    step = rows // chunks
    cut = [slice(i * step, (i + 1) * step) for i in range(chunks)]

    group_ids = jnp.arange(groups, dtype=jnp.int32)
    weights_f = mix_weights.astype(jnp.float32)
    own_partners = partners[own_group]
    own_weights = weights_f[own_group]
    total = jnp.sum(own_weights)
    row_coef = own_weights[0] * (group_ids == own_group).astype(jnp.float32)
    for slot in range(4):
        row_coef = row_coef + own_weights[slot + 1] * (group_ids == own_partners[slot]).astype(
            jnp.float32
        )
    row_coef = row_coef / total

    def others(s):
        delta = (master[s] - working[s].astype(jnp.float32)).astype(jnp.bfloat16)
        if groups == 2:
            return [lax.ppermute(delta, "replica", [(0, 1), (1, 0)])]
        every = lax.all_gather(delta, "replica", axis=0)
        return [every[g] for g in range(groups)]

    def update(master, momentum, working, received):
        delta = master - working.astype(jnp.float32)
        mixed = row_coef[own_group] * delta
        if groups == 2:
            mixed = mixed + row_coef[1 - own_group] * received[0].astype(jnp.float32)
        else:
            for g in range(groups):
                coef = jnp.where(own_group == g, 0.0, row_coef[g])
                mixed = mixed + coef * received[g].astype(jnp.float32)
        new_momentum = momentum_decay * momentum + mixed
        new_master = master - outer_rate * (mixed + momentum_decay * new_momentum)
        return new_master, new_momentum

    received = [others(s) for s in cut]

    if line == 4:
        order = [0, 1, 3, 2]
        order = jnp.stack([place ^ (k * PLANE + d) for k in order for d in range(PLANE)])
    else:
        order = jnp.stack([((place % PLANE) ^ d) + k * PLANE for k in range(line) for d in range(PLANE)])
    own, for_core, for_y, for_both = arrange_tokens(tokens, order.astype(jnp.int32), rows)
    from_y = lax.ppermute(for_y, "fsdp", plane_pairs(size, 2))
    at_core = lax.ppermute(for_both, "fsdp", plane_pairs(size, 1))
    from_core = lax.ppermute(for_core, "fsdp", plane_pairs(size, 1))
    from_both = lax.ppermute(at_core, "fsdp", plane_pairs(size, 2))
    inputs = [own, from_core, from_y, from_both]

    fresh = [
        update(master[s], momentum[s], working[s], r)[0].astype(jnp.bfloat16)
        for s, r in zip(cut, received)
    ]
    if line == 4:
        z = place // PLANE
        middle = (z == 1) | (z == 2)
        near, far, last = [], [], []
        for f in fresh:
            far.append(lax.ppermute(f, "fsdp", line_pairs(size, [3, 2, 1, 0])))
            near.append(lax.ppermute(f, "fsdp", line_pairs(size, [1, 0, 3, 2])))
        for f, g in zip(fresh, far):
            last.append(lax.ppermute(jnp.where(middle, g, f), "fsdp", line_pairs(size, [2, 0, 3, 1])))
        arrivals = [fresh, near, far, last]
    else:
        lines = [[k * PLANE + p for k in range(line)] for p in range(PLANE)]
        every = [lax.all_gather(f, "fsdp", axis=0, axis_index_groups=lines) for f in fresh]
        arrivals = [[e[k] for e in every] for k in range(line)]

    def partial_keys(t):
        return sum(
            product(t[:, k * rows + s.start : k * rows + s.stop], w)
            for k, block in enumerate(arrivals)
            for s, w in zip(cut, block)
        )

    own, from_core, from_y, from_both = [partial_keys(t) for t in inputs]
    back = lax.ppermute(jnp.concatenate([from_core, from_both]), "fsdp", plane_pairs(size, 1))
    count = own.shape[0]
    own = own + back[:count]
    to_y = (from_y + back[count:]).astype(jnp.bfloat16)
    keys = own + lax.ppermute(to_y, "fsdp", plane_pairs(size, 2)).astype(jnp.float32)

    full = [jnp.concatenate(list(r)) for r in zip(*received)]
    new_master, new_momentum = update(master, momentum, working, full)
    return new_master[None], new_momentum[None], keys.astype(jnp.bfloat16)[None]


def solution(mesh):
    return jax.shard_map(
        shards,
        mesh=mesh,
        in_specs=(
            P("replica", "fsdp", None),
            P("replica", "fsdp", None),
            P("replica", "fsdp", None),
            P("replica", "fsdp", None),
            P(),
            P(),
        ),
        out_specs=(
            P("replica", "fsdp", None),
            P("replica", "fsdp", None),
            P("replica", "fsdp", None),
        ),
        check_vma=False,
    )
```

```python
import functools

import jax
import jax.numpy as jnp
from jax import lax
from jax.experimental import pallas as pl
from jax.experimental.pallas import tpu as pltpu
from jax.sharding import PartitionSpec as P

outer_rate = 0.7
momentum_decay = 0.9
PLANE = 4
CHUNKS = 2
SMEM = pl.BlockSpec(memory_space=pltpu.SMEM)
SMALL = pltpu.CompilerParams(vmem_limit_bytes=16 * 2**20)
LITTLE = pl.CostEstimate(flops=0, bytes_accessed=0, transcendentals=0)


def plane_pairs(size, bit):
    return [(i, i ^ bit) for i in range(size)]


def line_pairs(size, to):
    return [(i, to[i // PLANE] * PLANE + i % PLANE) for i in range(size)]


def whole(array):
    return pl.BlockSpec(array.shape, lambda *_: (0,) * array.ndim)


def arrange_body(order, *refs):
    for source, target in zip(refs[:PLANE], refs[PLANE:]):
        target[...] = source[...]


def arrange_tokens(tokens, order, width):
    rows, blocks = tokens.shape[0], order.shape[0] // PLANE

    def column(distance):
        return lambda k, order: (0, order[k * PLANE + distance])

    return pl.pallas_call(
        arrange_body,
        grid_spec=pltpu.PrefetchScalarGridSpec(
            num_scalar_prefetch=1,
            grid=(blocks,),
            in_specs=[pl.BlockSpec((rows, width), column(d)) for d in range(PLANE)],
            out_specs=[pl.BlockSpec((rows, width), lambda k, order: (0, k))] * PLANE,
        ),
        out_shape=[jax.ShapeDtypeStruct((rows, blocks * width), tokens.dtype)] * PLANE,
        cost_estimate=LITTLE,
        compiler_params=SMALL,
        name="arrange_tokens",
    )(order, *([tokens] * PLANE))


def delta_body(master, working, delta):
    delta[...] = (master[...] - working[...].astype(jnp.float32)).astype(delta.dtype)


def pseudo_gradient(master, working, chunk, rows):
    block = pl.BlockSpec((rows, master.shape[1]), lambda *_: (chunk, 0))
    shape = (rows, master.shape[1])
    return pl.pallas_call(
        delta_body,
        grid=(1,),
        in_specs=[block, block],
        out_specs=pl.BlockSpec(shape, lambda *_: (0, 0)),
        out_shape=jax.ShapeDtypeStruct(shape, jnp.bfloat16),
        cost_estimate=LITTLE,
        compiler_params=SMALL,
        name="pseudo_gradient",
    )(master, working)


def update_body(groups, own_group, partners, mix_weights, master, momentum, working, *refs):
    received, outs = refs[: max(groups - 1, 1) if groups == 2 else groups], refs[-2:]
    me = own_group[0]
    numerators = [mix_weights[me, j].astype(jnp.float32) for j in range(5)]
    total = sum(numerators)

    def coefficient(group):
        found = jnp.where(group == me, numerators[0], 0.0)
        for j in range(4):
            found = found + jnp.where(partners[me, j] == group, numerators[j + 1], 0.0)
        return found

    mixed = coefficient(me) * (master[...] - working[...].astype(jnp.float32))
    if groups == 2:
        mixed = mixed + coefficient(1 - me) * received[0][...].astype(jnp.float32)
    else:
        for g in range(groups):
            away = jnp.where(g == me, 0.0, coefficient(g))
            mixed = mixed + away * received[g][...].astype(jnp.float32)
    mixed = mixed / total
    new_momentum = momentum_decay * momentum[...] + mixed
    new_master = master[...] - outer_rate * (mixed + momentum_decay * new_momentum)
    if len(refs) == len(received) + 1:
        refs[-1][...] = new_master.astype(jnp.bfloat16)
    else:
        outs[0][...] = new_master
        outs[1][...] = new_momentum


def next_working(scalars, groups, master, momentum, working, received, chunk, rows):
    width = master.shape[1]
    block = pl.BlockSpec((rows, width), lambda *_: (chunk, 0))
    return pl.pallas_call(
        functools.partial(update_body, groups),
        grid=(1,),
        in_specs=[SMEM] * 3 + [block] * 3 + [whole(r) for r in received],
        out_specs=pl.BlockSpec((rows, width), lambda *_: (0, 0)),
        out_shape=jax.ShapeDtypeStruct((rows, width), jnp.bfloat16),
        cost_estimate=LITTLE,
        compiler_params=SMALL,
        name="next_working",
    )(*scalars, master, momentum, working, *received)


def outer_step_body(groups, chunks, own_group, partners, mix_weights, master, momentum, working, *refs):
    received, outs = refs[:-2], refs[-2:]
    step = master.shape[0] // chunks
    each = len(received) // chunks
    for i in range(chunks):
        part = pl.ds(i * step, step)
        update_body(
            groups, own_group, partners, mix_weights, master.at[part], momentum.at[part], working.at[part],
            *received[i * each : (i + 1) * each], *[o.at[part] for o in outs],
        )


def outer_step(scalars, groups, master, momentum, working, received):
    received = [r for chunk in received for r in chunk]
    chunks = len(received) // (1 if groups == 2 else groups)
    shape = jax.ShapeDtypeStruct(master.shape, jnp.float32)
    return pl.pallas_call(
        functools.partial(outer_step_body, groups, chunks),
        grid=(1,),
        in_specs=[SMEM] * 3 + [whole(a) for a in (master, momentum, working, *received)],
        out_specs=[whole(master)] * 2,
        out_shape=[shape, shape],
        cost_estimate=LITTLE,
        compiler_params=SMALL,
        name="outer_step",
    )(*scalars, master, momentum, working, *received)


def product(tokens, pieces, offsets):
    total = None
    for piece, offset in zip(pieces, offsets):
        term = jnp.dot(
            tokens[:, offset : offset + piece.shape[0]], piece[...], preferred_element_type=jnp.float32
        )
        total = term if total is None else total + term
    return total


def early_body(offsets, tokens, *refs):
    refs[-1][...] = product(tokens, refs[:-1], offsets)


def early_keys(tokens, pieces, offsets):
    span = max(o + p.shape[0] for o, p in zip(offsets, pieces))
    rows, width = tokens.shape[0], pieces[0].shape[1]
    return pl.pallas_call(
        functools.partial(early_body, offsets),
        grid=(1,),
        in_specs=[pl.BlockSpec((rows, span), lambda *_: (0, 0))] + [whole(p) for p in pieces],
        out_specs=pl.BlockSpec((rows, width), lambda *_: (0, 0)),
        out_shape=jax.ShapeDtypeStruct((rows, width), jnp.float32),
        cost_estimate=LITTLE,
        compiler_params=SMALL,
        name="early_keys",
    )(tokens, *pieces)


def late_body(offsets, *refs):
    tokens, sums, pieces = refs[:PLANE], refs[PLANE : 2 * PLANE], refs[2 * PLANE : -3]
    own, from_core, from_y, from_both = [s[...] + product(t, pieces, offsets) for t, s in zip(tokens, sums)]
    keep, keep_y, to_core = refs[-3:]
    count = keep.shape[0]
    to_core[:count] = from_core
    to_core[count:] = from_both
    keep[...] = own
    keep_y[...] = from_y


def late_keys(tokens, sums, pieces, offsets):
    least, span = min(offsets), max(o + p.shape[0] for o, p in zip(offsets, pieces))
    rows, width = sums[0].shape
    if least % (span - least):
        least = 0
    taken = pl.BlockSpec((rows, span - least), lambda *_: (0, least // (span - least)))
    offsets = [o - least for o in offsets]
    one = jax.ShapeDtypeStruct((rows, width), jnp.float32)
    two = jax.ShapeDtypeStruct((2 * rows, width), jnp.float32)
    return pl.pallas_call(
        functools.partial(late_body, offsets),
        grid=(1,),
        in_specs=[taken] * PLANE + [whole(a) for a in (*sums, *pieces)],
        out_specs=[whole(one), whole(one), whole(two)],
        out_shape=[one, one, two],
        cost_estimate=LITTLE,
        compiler_params=SMALL,
        name="late_keys",
    )(*tokens, *sums, *pieces)


def over_core_body(keep_y, back, to_y):
    to_y[...] = (keep_y[...] + back[...]).astype(to_y.dtype)


def over_core(keep_y, back):
    rows, width = keep_y.shape
    return pl.pallas_call(
        over_core_body,
        grid=(1,),
        in_specs=[whole(keep_y), pl.BlockSpec((rows, width), lambda *_: (1, 0))],
        out_specs=whole(keep_y),
        out_shape=jax.ShapeDtypeStruct((rows, width), jnp.bfloat16),
        cost_estimate=LITTLE,
        compiler_params=SMALL,
        name="over_core",
    )(keep_y, back)


def over_y_body(keep, back, there, keys):
    keys[...] = (keep[...] + back[...] + there[...].astype(jnp.float32)).astype(keys.dtype)


def over_y(keep, back, there):
    rows, width = keep.shape
    return pl.pallas_call(
        over_y_body,
        grid=(1,),
        in_specs=[whole(keep), pl.BlockSpec((rows, width), lambda *_: (0, 0)), whole(there)],
        out_specs=whole(keep),
        out_shape=jax.ShapeDtypeStruct((rows, width), jnp.bfloat16),
        cost_estimate=LITTLE,
        compiler_params=SMALL,
        name="over_y",
    )(keep, back, there)


def shards(master, momentum, working, tokens, partners, mix_weights):
    groups = lax.axis_size("replica")
    size = lax.axis_size("fsdp")
    line = size // PLANE
    place = lax.axis_index("fsdp")
    master, momentum, working, tokens = master[0], momentum[0], working[0], tokens[0]
    rows = master.shape[0]
    chunks = CHUNKS if rows % (CHUNKS * 16) == 0 else 1
    step = rows // chunks
    scalars = (lax.axis_index("replica").astype(jnp.int32)[None], partners, mix_weights)

    received = []
    for i in range(chunks):
        delta = pseudo_gradient(master, working, i, step)
        if groups == 2:
            received.append([lax.ppermute(delta, "replica", [(0, 1), (1, 0)])])
        else:
            every = lax.all_gather(delta, "replica", axis=0)
            received.append([every[g] for g in range(groups)])

    if line == 4:
        order = [place ^ (k * PLANE + d) for k in (0, 1, 3, 2) for d in range(PLANE)]
    else:
        order = [((place % PLANE) ^ d) + k * PLANE for k in range(line) for d in range(PLANE)]
    order = jnp.stack(order).astype(jnp.int32)
    own, for_core, for_y, for_both = arrange_tokens(tokens, order, rows)
    from_y = lax.ppermute(for_y, "fsdp", plane_pairs(size, 2))
    at_core = lax.ppermute(for_both, "fsdp", plane_pairs(size, 1))
    from_core = lax.ppermute(for_core, "fsdp", plane_pairs(size, 1))
    from_both = lax.ppermute(at_core, "fsdp", plane_pairs(size, 2))
    inputs = [own, from_core, from_y, from_both]

    fresh = [
        next_working(scalars, groups, master, momentum, working, received[i], i, step) for i in range(chunks)
    ]
    if line == 4:
        z = place // PLANE
        middle = (z == 1) | (z == 2)
        far = [lax.ppermute(f, "fsdp", line_pairs(size, [3, 2, 1, 0])) for f in fresh]
        near = [lax.ppermute(f, "fsdp", line_pairs(size, [1, 0, 3, 2])) for f in fresh]
        last = [
            lax.ppermute(jnp.where(middle, g, f), "fsdp", line_pairs(size, [2, 0, 3, 1]))
            for f, g in zip(fresh, far)
        ]
        early, late = [*fresh, *near, *far], last
    else:
        lines = [[k * PLANE + p for k in range(line)] for p in range(PLANE)]
        every = [lax.all_gather(f, "fsdp", axis=0, axis_index_groups=lines) for f in fresh]
        blocks = [e[k] for k in range(line) for e in every]
        early, late = blocks[:-chunks], blocks[-chunks:]
    offsets = [i * step for i in range(line * chunks)]

    sums = [early_keys(t, early, offsets[:-chunks]) for t in inputs]
    keep, keep_y, to_core = late_keys(inputs, sums, late, offsets[-chunks:])
    back = lax.ppermute(to_core, "fsdp", plane_pairs(size, 1))
    there = lax.ppermute(over_core(keep_y, back), "fsdp", plane_pairs(size, 2))
    keys = over_y(keep, back, there)

    new_master, new_momentum = outer_step(scalars, groups, master, momentum, working, received)
    return new_master[None], new_momentum[None], keys[None]


def solution(mesh):
    return jax.shard_map(
        shards,
        mesh=mesh,
        in_specs=(
            P("replica", "fsdp", None),
            P("replica", "fsdp", None),
            P("replica", "fsdp", None),
            P("replica", "fsdp", None),
            P(),
            P(),
        ),
        out_specs=(
            P("replica", "fsdp", None),
            P("replica", "fsdp", None),
            P("replica", "fsdp", None),
        ),
        check_vma=False,
    )
```

```python
import functools

import jax
import jax.numpy as jnp
from jax import lax
from jax.experimental import pallas as pl
from jax.experimental.pallas import tpu as pltpu
from jax.sharding import PartitionSpec as P

outer_rate = 0.7
momentum_decay = 0.9
PLANE = 4
FIRST = 8
HBM = pl.BlockSpec(memory_space=pltpu.HBM)
SMEM = pl.BlockSpec(memory_space=pltpu.SMEM)
LARGE = pltpu.CompilerParams(vmem_limit_bytes=60 * 2**20)
SMALL = pltpu.CompilerParams(vmem_limit_bytes=16 * 2**20)


def cost(us):
    return pl.CostEstimate(flops=int(us * 1_153_000_000), bytes_accessed=0, transcendentals=0)


COST = dict(add_keys=1, pick=3)


def plane_pairs(size, bit):
    return [(i, i ^ bit) for i in range(size)]


def line_pairs(size, to):
    return [(i, to[i // PLANE] * PLANE + i % PLANE) for i in range(size)]


def whole(array):
    return pl.BlockSpec(array.shape, lambda *_: (0,) * array.ndim)


def arrange_body(width, distances, order, tokens, *refs):
    count = len(distances)
    outs, held, (arrived, left) = refs[:count], refs[count : 2 * count], refs[2 * count :]
    blocks = outs[0].shape[1] // width
    copies = []
    for i, distance in enumerate(distances):
        for k in range(blocks):
            start = pl.multiple_of(order[k * PLANE + distance] * width, width)
            copies.append(
                pltpu.make_async_copy(
                    tokens.at[:, pl.ds(start, width)],
                    held[i].at[:, pl.ds(k * width, width)],
                    arrived.at[i * blocks + k],
                )
            )
    for copy in copies:
        copy.start()
    away = [pltpu.make_async_copy(held[i], outs[i], left.at[i]) for i in range(count)]
    for i in range(count):
        for k in range(blocks):
            copies[i * blocks + k].wait()
        away[i].start()
    for copy in away:
        copy.wait()


def arrange_tokens(tokens, order, width, distances):
    blocks = order.shape[0] // PLANE
    shape = (tokens.shape[0], blocks * width)
    return pl.pallas_call(
        functools.partial(arrange_body, width, distances),
        grid=(1,),
        in_specs=[SMEM, HBM],
        out_specs=[HBM] * len(distances),
        out_shape=[jax.ShapeDtypeStruct(shape, tokens.dtype)] * len(distances),
        scratch_shapes=[pltpu.VMEM(shape, tokens.dtype)] * len(distances)
        + [pltpu.SemaphoreType.DMA((blocks * len(distances),)), pltpu.SemaphoreType.DMA((len(distances),))],
        cost_estimate=cost(0),
        compiler_params=LARGE,
        name="arrange_tokens",
    )(order, tokens)


def mixing_body(groups, own_group, partners, mix_weights, row):
    me = own_group[0]
    numerators = [mix_weights[me, j].astype(jnp.float32) for j in range(5)]
    total = sum(numerators)

    def coefficient(group):
        found = jnp.where(group == me, numerators[0], 0.0)
        for j in range(4):
            found = found + jnp.where(partners[me, j] == group, numerators[j + 1], 0.0)
        return jnp.full((1, row.shape[1]), found / total, jnp.float32)

    row[0:1] = coefficient(me)
    if groups == 2:
        row[1:2] = coefficient(1 - me)
    else:
        for g in range(groups):
            row[g + 1 : g + 2] = jnp.where(g == me, 0.0, coefficient(g))


def mixing_row(groups, *scalars):
    shape = (-(-(groups + 1) // 8) * 8, 128)
    row = pl.pallas_call(
        functools.partial(mixing_body, groups),
        grid=(1,),
        in_specs=[SMEM] * 3,
        out_specs=pl.BlockSpec(shape, lambda *_: (0, 0)),
        out_shape=jax.ShapeDtypeStruct(shape, jnp.float32),
        cost_estimate=cost(0),
        compiler_params=SMALL,
        name="mixing_row",
    )(*scalars)
    return row[:, 0]


def delta_body(starts, master, working, *refs):
    outs, (master_here, working_here, arrived) = refs[:-3], refs[-3:]
    copies = []
    for i, (start, out) in enumerate(zip(starts, outs)):
        part = pl.ds(start, out.shape[0])
        copies.append(
            [
                pltpu.make_async_copy(there.at[part], here.at[part], arrived.at[i, j])
                for j, (there, here) in enumerate([(master, master_here), (working, working_here)])
            ]
        )
    for copy in sum(copies, []):
        copy.start()
    for start, out, pair in zip(starts, outs, copies):
        part = slice(start, start + out.shape[0])
        for copy in pair:
            copy.wait()
        out[...] = (master_here[part] - working_here[part].astype(jnp.float32)).astype(out.dtype)


def pseudo_gradient(master, working, cuts):
    shapes = [(size, master.shape[1]) for _, size in cuts]
    return pl.pallas_call(
        functools.partial(delta_body, [start for start, _ in cuts]),
        grid=(1,),
        in_specs=[HBM, HBM],
        out_specs=[pl.BlockSpec(shape, lambda *_: (0, 0)) for shape in shapes],
        out_shape=[jax.ShapeDtypeStruct(shape, jnp.bfloat16) for shape in shapes],
        scratch_shapes=[
            pltpu.VMEM(master.shape, master.dtype),
            pltpu.VMEM(working.shape, working.dtype),
            pltpu.SemaphoreType.DMA((len(cuts), 2)),
        ],
        cost_estimate=cost(0),
        compiler_params=LARGE,
        name="pseudo_gradient",
    )(master, working)


def outer_step(row, master, momentum, working, received):
    mixed = row[0] * (master - working.astype(jnp.float32))
    for i, other in enumerate(received):
        mixed = mixed + row[i + 1] * other.astype(jnp.float32)
    new_momentum = momentum_decay * momentum + mixed
    new_master = master - outer_rate * (mixed + momentum_decay * new_momentum)
    return new_master, new_momentum


def after(value, *others):
    return lax.optimization_barrier((value, *others))[0]


def product(tokens, pieces, offsets):
    total = None
    for piece, offset in zip(pieces, offsets):
        term = jnp.dot(
            tokens[:, offset : offset + piece.shape[0]], piece[...], preferred_element_type=jnp.float32
        )
        total = term if total is None else total + term
    return total


def early_body(offsets, tokens, *refs):
    refs[-1][...] = product(tokens, refs[:-1], offsets)


def early_keys(tokens, pieces, offsets):
    span = max(o + p.shape[0] for o, p in zip(offsets, pieces))
    rows, width = tokens.shape[0], pieces[0].shape[1]
    return pl.pallas_call(
        functools.partial(early_body, offsets),
        grid=(1,),
        in_specs=[pl.BlockSpec((rows, span), lambda *_: (0, 0))] + [whole(p) for p in pieces],
        out_specs=pl.BlockSpec((rows, width), lambda *_: (0, 0)),
        out_shape=jax.ShapeDtypeStruct((rows, width), jnp.float32),
        cost_estimate=cost(0),
        compiler_params=SMALL,
        name="early_keys",
    )(tokens, *pieces)


def last_block(tokens, width):
    rows, span = tokens.shape
    return pl.BlockSpec((rows, width), lambda *_: (0, span // width - 1))


def add_body(offset, *refs):
    tokens, sums, piece, outs = refs[:PLANE], refs[PLANE : 2 * PLANE], refs[2 * PLANE], refs[-PLANE:]
    for t, s, o in zip(tokens, sums, outs):
        o[...] = s[...] + product(t, [piece], [offset])


def add_keys(tokens, sums, width, piece, offset):
    rows, columns = sums[0].shape
    return pl.pallas_call(
        functools.partial(add_body, offset),
        grid=(1,),
        in_specs=[last_block(t, width) for t in tokens] + [whole(a) for a in (*sums, piece)],
        out_specs=[whole(s) for s in sums],
        out_shape=[jax.ShapeDtypeStruct((rows, columns), jnp.float32)] * PLANE,
        cost_estimate=cost(COST["add_keys"]),
        compiler_params=SMALL,
        name="add_keys",
    )(*tokens, *sums, piece)


def pick_body(own_first, own, passed, *refs):
    @pl.when(own_first[0] == 1)
    def _():
        refs[-1][...] = own[...]

    @pl.when(own_first[0] == 0)
    def _():
        refs[-1][...] = passed[...]


def pick(own_first, own, passed):
    return pl.pallas_call(
        pick_body,
        grid=(1,),
        in_specs=[SMEM, whole(own), whole(passed)],
        out_specs=whole(own),
        out_shape=jax.ShapeDtypeStruct(own.shape, own.dtype),
        cost_estimate=cost(COST["pick"]),
        compiler_params=SMALL,
        name="pick",
    )(own_first, own, passed)


def late_body(offset, *refs):
    tokens, sums, piece, (keep, keep_y, to_core) = refs[:PLANE], refs[PLANE:-4], refs[-4], refs[-3:]
    own, from_core, from_y, from_both = [s[...] + product(t, [piece], [offset]) for t, s in zip(tokens, sums)]
    count = keep.shape[0]
    to_core[:count] = from_core
    to_core[count:] = from_both
    keep[...] = own
    keep_y[...] = from_y


def late_keys(tokens, sums, width, piece, offset):
    rows, columns = sums[0].shape
    one = jax.ShapeDtypeStruct((rows, columns), jnp.float32)
    two = jax.ShapeDtypeStruct((2 * rows, columns), jnp.float32)
    return pl.pallas_call(
        functools.partial(late_body, offset),
        grid=(1,),
        in_specs=[last_block(t, width) for t in tokens] + [whole(a) for a in (*sums, piece)],
        out_specs=[whole(one), whole(one), whole(two)],
        out_shape=[one, one, two],
        cost_estimate=cost(0),
        compiler_params=SMALL,
        name="late_keys",
    )(*tokens, *sums, piece)


def over_core_body(keep_y, back, to_y):
    to_y[...] = (keep_y[...] + back[...]).astype(to_y.dtype)


def over_core(keep_y, back):
    rows, width = keep_y.shape
    return pl.pallas_call(
        over_core_body,
        grid=(1,),
        in_specs=[whole(keep_y), pl.BlockSpec((rows, width), lambda *_: (1, 0))],
        out_specs=whole(keep_y),
        out_shape=jax.ShapeDtypeStruct((rows, width), jnp.bfloat16),
        cost_estimate=cost(0),
        compiler_params=SMALL,
        name="over_core",
    )(keep_y, back)


def over_y_body(keep, back, there, keys):
    keys[...] = (keep[...] + back[...] + there[...].astype(jnp.float32)).astype(keys.dtype)


def over_y(keep, back, there):
    rows, width = keep.shape
    return pl.pallas_call(
        over_y_body,
        grid=(1,),
        in_specs=[whole(keep), pl.BlockSpec((rows, width), lambda *_: (0, 0)), whole(there)],
        out_specs=whole(keep),
        out_shape=jax.ShapeDtypeStruct((rows, width), jnp.bfloat16),
        cost_estimate=cost(0),
        compiler_params=SMALL,
        name="over_y",
    )(keep, back, there)


def shards(master, momentum, working, tokens, partners, mix_weights):
    groups = lax.axis_size("replica")
    size = lax.axis_size("fsdp")
    line = size // PLANE
    place = lax.axis_index("fsdp")
    master, momentum, working, tokens = master[0], momentum[0], working[0], tokens[0]
    rows = master.shape[0]
    first = rows * FIRST // 16
    cuts = [(0, first), (first, rows - first)]
    parts = [slice(start, start + count) for start, count in cuts]

    deltas = pseudo_gradient(master, working, cuts)
    received = []
    for delta in deltas:
        if groups == 2:
            received.append([lax.ppermute(delta, "replica", [(0, 1), (1, 0)])])
        else:
            every = lax.all_gather(delta, "replica", axis=0)
            received.append([every[g] for g in range(groups)])
    row = mixing_row(groups, lax.axis_index("replica").astype(jnp.int32)[None], partners, mix_weights)

    if line == 4:
        order = [place ^ (k * PLANE + d) for k in (0, 1, 3, 2) for d in range(PLANE)]
    else:
        order = [((place % PLANE) ^ d) + k * PLANE for k in range(line) for d in range(PLANE)]
    order = after(jnp.stack(order).astype(jnp.int32), *deltas)
    for_y, for_both, for_core, own = arrange_tokens(tokens, order, rows, [2, 3, 1, 0])
    from_y = lax.ppermute(for_y, "fsdp", plane_pairs(size, 2))
    at_core = lax.ppermute(for_both, "fsdp", plane_pairs(size, 1))
    from_core = lax.ppermute(for_core, "fsdp", plane_pairs(size, 1))

    fresh = []
    for part, there in zip(parts, received):
        there = [after(t, *fresh) for t in there]
        new_master, _ = outer_step(row, master[part], momentum[part], working[part], there)
        fresh.append(new_master.astype(jnp.bfloat16))
    if line == 4:
        z = place // PLANE
        own_first = jnp.where((z == 1) | (z == 2), 0, 1).astype(jnp.int32)[None]
        far = [lax.ppermute(f, "fsdp", line_pairs(size, [3, 2, 1, 0])) for f in fresh]
        ready = [after(fresh[0], at_core, from_core), fresh[1]]
        near = [lax.ppermute(f, "fsdp", line_pairs(size, [1, 0, 3, 2])) for f in ready]
        passed = [far[0], far[1]]
        last = [
            lax.ppermute(pick(own_first, f, g), "fsdp", line_pairs(size, [2, 0, 3, 1]))
            for f, g in zip(fresh, passed)
        ]
        blocks = [fresh, near, far, last]
    else:
        lines = [[k * PLANE + p for k in range(line)] for p in range(PLANE)]
        every = [lax.all_gather(f, "fsdp", axis=0, axis_index_groups=lines) for f in fresh]
        blocks = [[e[k] for e in every] for k in range(line)]

    from_both = lax.ppermute(after(at_core, from_y, from_core), "fsdp", plane_pairs(size, 2))
    inputs = [own, from_core, from_y, from_both]

    early = [piece for block in blocks[:-1] for piece in block]
    offsets = [k * rows + start for k in range(line - 1) for start, _ in cuts]
    sums = [early_keys(t, early, offsets) for t in inputs]
    sums = add_keys(inputs, sums, rows, blocks[-1][0], cuts[0][0])
    keep, keep_y, to_core = late_keys(inputs, sums, rows, blocks[-1][1], cuts[1][0])
    back = lax.ppermute(to_core, "fsdp", plane_pairs(size, 1))
    there = lax.ppermute(over_core(keep_y, back), "fsdp", plane_pairs(size, 2))
    keys = over_y(keep, back, there)

    received = [after(jnp.concatenate(list(r)), keep) for r in zip(*received)]
    new_master, new_momentum = outer_step(row, master, momentum, working, received)
    return new_master[None], new_momentum[None], keys[None]


def solution(mesh):
    return jax.shard_map(
        shards,
        mesh=mesh,
        in_specs=(
            P("replica", "fsdp", None),
            P("replica", "fsdp", None),
            P("replica", "fsdp", None),
            P("replica", "fsdp", None),
            P(),
            P(),
        ),
        out_specs=(
            P("replica", "fsdp", None),
            P("replica", "fsdp", None),
            P("replica", "fsdp", None),
        ),
        check_vma=False,
    )
```

```python
import functools

import jax
import jax.numpy as jnp
from jax import lax
from jax.experimental import pallas as pl
from jax.experimental.pallas import tpu as pltpu
from jax.sharding import PartitionSpec as P

outer_rate = 0.7
momentum_decay = 0.9
PLANE = 4
FIRST = 8
HBM = pl.BlockSpec(memory_space=pltpu.HBM)
SMEM = pl.BlockSpec(memory_space=pltpu.SMEM)
FIRST_LIMIT = pltpu.CompilerParams(vmem_limit_bytes=int(60 * 2**20))
ARRANGE_LIMIT = pltpu.CompilerParams(vmem_limit_bytes=int(60 * 2**20))
SMALL = pltpu.CompilerParams(vmem_limit_bytes=16 * 2**20)


def cost(us):
    return pl.CostEstimate(flops=int(us * 1_153_000_000), bytes_accessed=0, transcendentals=0)


COST = dict(add_keys=1, pick=4.5, next_working=4)


def plane_pairs(size, bit):
    return [(i, i ^ bit) for i in range(size)]


def line_pairs(size, to):
    return [(i, to[i // PLANE] * PLANE + i % PLANE) for i in range(size)]


def whole(array):
    return pl.BlockSpec(array.shape, lambda *_: (0,) * array.ndim)


def block_of(line, place, k, distance):
    if line == 4:
        return place ^ ([0, 1, 3, 2][k] * PLANE + distance)
    return ((place % PLANE) ^ distance) + k * PLANE


def arrange_body(width, distances, place, tokens, *refs):
    count = len(distances)
    outs, held, (arrived, left) = refs[:count], refs[count : 2 * count], refs[2 * count :]
    line = outs[0].shape[1] // width
    copies = []
    for i, distance in enumerate(distances):
        for k in range(line):
            start = pl.multiple_of(block_of(line, place[0], k, distance) * width, width)
            copies.append(
                pltpu.make_async_copy(
                    tokens.at[:, pl.ds(start, width)],
                    held[i].at[:, pl.ds(k * width, width)],
                    arrived.at[i * line + k],
                )
            )
    for copy in copies:
        copy.start()
    away = [pltpu.make_async_copy(held[i], outs[i], left.at[i]) for i in range(count)]
    for i in range(count):
        for k in range(line):
            copies[i * line + k].wait()
        away[i].start()
    for copy in away:
        copy.wait()


def arrange_tokens(place, tokens, line, width, distances):
    shape = (tokens.shape[0], line * width)
    return pl.pallas_call(
        functools.partial(arrange_body, width, distances),
        grid=(1,),
        in_specs=[SMEM, HBM],
        out_specs=[HBM] * len(distances),
        out_shape=[jax.ShapeDtypeStruct(shape, tokens.dtype)] * len(distances),
        scratch_shapes=[pltpu.VMEM(shape, tokens.dtype)] * len(distances)
        + [pltpu.SemaphoreType.DMA((line * len(distances),)), pltpu.SemaphoreType.DMA((len(distances),))],
        cost_estimate=cost(0),
        compiler_params=ARRANGE_LIMIT,
        name="arrange_tokens",
    )(place, tokens)


def read_mixing(own_group, partners, mix_weights):
    me = own_group[0]
    numerators = [mix_weights[me, j].astype(jnp.float32) for j in range(5)]
    total = sum(numerators)

    def coefficient(group):
        found = jnp.where(group == me, numerators[0], 0.0)
        for j in range(4):
            found = found + jnp.where(partners[me, j] == group, numerators[j + 1], 0.0)
        return found / total

    return me, coefficient


def others_mixed(groups, me, coefficient, received):
    if groups == 2:
        return coefficient(1 - me) * received[0][...].astype(jnp.float32)
    mixed = jnp.zeros(received[0].shape, jnp.float32)
    for g in range(groups):
        mixed = mixed + jnp.where(g == me, 0.0, coefficient(g)) * received[g][...].astype(jnp.float32)
    return mixed


def first_body(starts, own_group, partners, mix_weights, master, momentum, working, *refs):
    outs, (master_here, momentum_here, working_here, arrived) = refs[:-4], refs[-4:]
    deltas, bases = outs[: len(starts)], outs[len(starts) :]
    parts = [pl.ds(start, delta.shape[0]) for start, delta in zip(starts, deltas)]
    copies = [
        [
            pltpu.make_async_copy(there.at[part], here.at[part], arrived.at[i, j])
            for i, part in enumerate(parts)
        ]
        for j, (there, here) in enumerate([(master, master_here), (working, working_here), (momentum, momentum_here)])
    ]
    for i in range(len(parts)):
        copies[0][i].start()
        copies[1][i].start()
    for i in range(len(parts)):
        copies[2][i].start()
    me, coefficient = read_mixing(own_group, partners, mix_weights)
    own = coefficient(me)
    for i, part in enumerate(parts):
        copies[0][i].wait()
        copies[1][i].wait()
        delta = master_here[part] - working_here[part].astype(jnp.float32)
        deltas[i][...] = delta.astype(jnp.bfloat16)
    for i, part in enumerate(parts):
        copies[2][i].wait()
        mixed = own * (master_here[part] - working_here[part].astype(jnp.float32))
        new_momentum = momentum_decay * momentum_here[part] + mixed
        bases[i][...] = master_here[part] - outer_rate * (mixed + momentum_decay * new_momentum)


def first_step(scalars, master, momentum, working, cuts):
    shapes = [(size, master.shape[1]) for _, size in cuts]
    outs = pl.pallas_call(
        functools.partial(first_body, [start for start, _ in cuts]),
        grid=(1,),
        in_specs=[SMEM] * 3 + [HBM] * 3,
        out_specs=[pl.BlockSpec(shape, lambda *_: (0, 0)) for shape in shapes] * 2,
        out_shape=[jax.ShapeDtypeStruct(shape, jnp.bfloat16) for shape in shapes]
        + [jax.ShapeDtypeStruct(shape, jnp.float32) for shape in shapes],
        scratch_shapes=[
            pltpu.VMEM(master.shape, master.dtype),
            pltpu.VMEM(momentum.shape, momentum.dtype),
            pltpu.VMEM(working.shape, working.dtype),
            pltpu.SemaphoreType.DMA((len(cuts), 3)),
        ],
        cost_estimate=cost(0),
        compiler_params=FIRST_LIMIT,
        name="first_step",
    )(*scalars, master, momentum, working)
    return outs[: len(cuts)], outs[len(cuts) :]


def working_body(groups, own_group, partners, mix_weights, base, *refs):
    me, coefficient = read_mixing(own_group, partners, mix_weights)
    mixed = others_mixed(groups, me, coefficient, refs)
    refs[-1][...] = (base[...] - outer_rate * (1 + momentum_decay) * mixed).astype(jnp.bfloat16)


def next_working(scalars, groups, base, received):
    return pl.pallas_call(
        functools.partial(working_body, groups),
        grid=(1,),
        in_specs=[SMEM] * 3 + [whole(a) for a in (base, *received)],
        out_specs=whole(base),
        out_shape=jax.ShapeDtypeStruct(base.shape, jnp.bfloat16),
        cost_estimate=cost(COST["next_working"]),
        compiler_params=SMALL,
        name="next_working",
    )(*scalars, base, *received)


def outer_step_body(groups, starts, own_group, partners, mix_weights, master, momentum, working, *refs):
    received, (new_master, new_momentum) = refs[:-2], refs[-2:]
    each = len(received) // len(starts)
    me, coefficient = read_mixing(own_group, partners, mix_weights)
    own = coefficient(me)
    for i, start in enumerate(starts):
        others = received[i * each : (i + 1) * each]
        part = slice(start, start + others[0].shape[0])
        mixed = own * (master[part] - working[part].astype(jnp.float32))
        mixed = mixed + others_mixed(groups, me, coefficient, others)
        momentum_now = momentum_decay * momentum[part] + mixed
        new_momentum[part] = momentum_now
        new_master[part] = master[part] - outer_rate * (mixed + momentum_decay * momentum_now)


def outer_step(scalars, groups, master, momentum, working, cuts, received):
    shape = jax.ShapeDtypeStruct(master.shape, jnp.float32)
    return pl.pallas_call(
        functools.partial(outer_step_body, groups, [start for start, _ in cuts]),
        grid=(1,),
        in_specs=[SMEM] * 3 + [whole(a) for a in (master, momentum, working, *received)],
        out_specs=[whole(master)] * 2,
        out_shape=[shape, shape],
        cost_estimate=cost(0),
        compiler_params=SMALL,
        name="outer_step",
    )(*scalars, master, momentum, working, *received)


def after(value, *others):
    return lax.optimization_barrier((value, *others))[0]


def product(tokens, pieces, offsets):
    total = None
    for piece, offset in zip(pieces, offsets):
        term = jnp.dot(
            tokens[:, offset : offset + piece.shape[0]], piece[...], preferred_element_type=jnp.float32
        )
        total = term if total is None else total + term
    return total


def early_body(offsets, tokens, *refs):
    refs[-1][...] = product(tokens, refs[:-1], offsets)


def early_keys(tokens, pieces, offsets):
    span = max(o + p.shape[0] for o, p in zip(offsets, pieces))
    rows, width = tokens.shape[0], pieces[0].shape[1]
    return pl.pallas_call(
        functools.partial(early_body, offsets),
        grid=(1,),
        in_specs=[pl.BlockSpec((rows, span), lambda *_: (0, 0))] + [whole(p) for p in pieces],
        out_specs=pl.BlockSpec((rows, width), lambda *_: (0, 0)),
        out_shape=jax.ShapeDtypeStruct((rows, width), jnp.float32),
        cost_estimate=cost(0),
        compiler_params=SMALL,
        name="early_keys",
    )(tokens, *pieces)


def last_block(tokens, width):
    rows, span = tokens.shape
    return pl.BlockSpec((rows, width), lambda *_: (0, span // width - 1))


def add_body(offset, *refs):
    tokens, sums, piece, outs = refs[:PLANE], refs[PLANE : 2 * PLANE], refs[2 * PLANE], refs[-PLANE:]
    for t, s, o in zip(tokens, sums, outs):
        o[...] = s[...] + product(t, [piece], [offset])


def add_keys(tokens, sums, width, piece, offset):
    rows, columns = sums[0].shape
    return pl.pallas_call(
        functools.partial(add_body, offset),
        grid=(1,),
        in_specs=[last_block(t, width) for t in tokens] + [whole(a) for a in (*sums, piece)],
        out_specs=[whole(s) for s in sums],
        out_shape=[jax.ShapeDtypeStruct((rows, columns), jnp.float32)] * PLANE,
        cost_estimate=cost(COST["add_keys"]),
        compiler_params=SMALL,
        name="add_keys",
    )(*tokens, *sums, piece)


def pick_body(own_first, own, passed, *refs):
    @pl.when(own_first[0] == 1)
    def _():
        refs[-1][...] = own[...]

    @pl.when(own_first[0] == 0)
    def _():
        refs[-1][...] = passed[...]


def pick(own_first, own, passed):
    return pl.pallas_call(
        pick_body,
        grid=(1,),
        in_specs=[SMEM, whole(own), whole(passed)],
        out_specs=whole(own),
        out_shape=jax.ShapeDtypeStruct(own.shape, own.dtype),
        cost_estimate=cost(COST["pick"]),
        compiler_params=SMALL,
        name="pick",
    )(own_first, own, passed)


def late_body(offset, *refs):
    tokens, sums, piece, outs = refs[:PLANE], refs[PLANE:-5], refs[-5], refs[-4:]
    for t, s, out in zip(tokens, sums, outs):
        out[...] = s[...] + product(t, [piece], [offset])


def late_keys(tokens, sums, width, piece, offset):
    rows, columns = sums[0].shape
    return pl.pallas_call(
        functools.partial(late_body, offset),
        grid=(1,),
        in_specs=[last_block(t, width) for t in tokens] + [whole(a) for a in (*sums, piece)],
        out_specs=[whole(s) for s in sums],
        out_shape=[jax.ShapeDtypeStruct((rows, columns), jnp.float32)] * PLANE,
        cost_estimate=cost(0),
        compiler_params=SMALL,
        name="late_keys",
    )(*tokens, *sums, piece)


def over_core_body(keep_y, back, to_y):
    to_y[...] = (keep_y[...] + back[...]).astype(to_y.dtype)


def over_core(keep_y, back):
    rows, width = keep_y.shape
    return pl.pallas_call(
        over_core_body,
        grid=(1,),
        in_specs=[whole(keep_y), whole(back)],
        out_specs=whole(keep_y),
        out_shape=jax.ShapeDtypeStruct((rows, width), jnp.bfloat16),
        cost_estimate=cost(0),
        compiler_params=SMALL,
        name="over_core",
    )(keep_y, back)


def over_y_body(keep, back, there, keys):
    keys[...] = (keep[...] + back[...] + there[...].astype(jnp.float32)).astype(keys.dtype)


def over_y(keep, back, there):
    rows, width = keep.shape
    return pl.pallas_call(
        over_y_body,
        grid=(1,),
        in_specs=[whole(keep), whole(back), whole(there)],
        out_specs=whole(keep),
        out_shape=jax.ShapeDtypeStruct((rows, width), jnp.bfloat16),
        cost_estimate=cost(0),
        compiler_params=SMALL,
        name="over_y",
    )(keep, back, there)


def shards(master, momentum, working, tokens, partners, mix_weights):
    groups = lax.axis_size("replica")
    size = lax.axis_size("fsdp")
    line = size // PLANE
    place = lax.axis_index("fsdp").astype(jnp.int32)[None]
    scalars = (lax.axis_index("replica").astype(jnp.int32)[None], partners, mix_weights)
    master, momentum, working, tokens = master[0], momentum[0], working[0], tokens[0]
    rows = master.shape[0]
    first = rows * FIRST // 16
    cuts = [(0, first), (first, rows - first)]

    deltas, bases = first_step(scalars, master, momentum, working, cuts)
    received = []
    for delta in deltas:
        if groups == 2:
            received.append([lax.ppermute(delta, "replica", [(0, 1), (1, 0)])])
        else:
            every = lax.all_gather(delta, "replica", axis=0)
            received.append([every[g] for g in range(groups)])

    for_y, for_both, for_core, own = arrange_tokens(after(place, *deltas), tokens, line, rows, [2, 3, 1, 0])
    from_y = lax.ppermute(for_y, "fsdp", plane_pairs(size, 2))
    at_core = lax.ppermute(for_both, "fsdp", plane_pairs(size, 1))
    from_core = lax.ppermute(for_core, "fsdp", plane_pairs(size, 1))

    fresh = []
    for base, there in zip(bases, received):
        fresh.append(next_working(scalars, groups, base, [after(t, *fresh) for t in there]))
    if line == 4:
        z = place // PLANE
        own_first = jnp.where((z == 1) | (z == 2), 0, 1).astype(jnp.int32)
        far = [lax.ppermute(f, "fsdp", line_pairs(size, [3, 2, 1, 0])) for f in fresh]
        ready = [after(fresh[0], at_core, from_core), fresh[1]]
        near = [lax.ppermute(f, "fsdp", line_pairs(size, [1, 0, 3, 2])) for f in ready]
        passed = [far[0], far[1]]
        last = [
            lax.ppermute(pick(own_first, f, g), "fsdp", line_pairs(size, [2, 0, 3, 1]))
            for f, g in zip(fresh, passed)
        ]
        blocks = [fresh, near, far, last]
    else:
        lines = [[k * PLANE + p for k in range(line)] for p in range(PLANE)]
        every = [lax.all_gather(f, "fsdp", axis=0, axis_index_groups=lines) for f in fresh]
        blocks = [[e[k] for e in every] for k in range(line)]
    from_both = lax.ppermute(after(at_core, from_y, from_core), "fsdp", plane_pairs(size, 2))
    inputs = [own, from_core, from_y, from_both]

    early = [piece for block in blocks[:-1] for piece in block]
    offsets = [k * rows + start for k in range(line - 1) for start, _ in cuts]
    sums = [early_keys(t, early, offsets) for t in inputs]
    sums = add_keys(inputs, sums, rows, blocks[-1][0], cuts[0][0])
    own, for_core, keep_y, for_both = late_keys(inputs, sums, rows, blocks[-1][1], cuts[1][0])
    to_y = over_core(keep_y, lax.ppermute(for_both, "fsdp", plane_pairs(size, 1)))
    back = lax.ppermute(for_core, "fsdp", plane_pairs(size, 1))
    keys = over_y(own, back, lax.ppermute(to_y, "fsdp", plane_pairs(size, 2)))

    received = [after(r, to_y) for chunk in received for r in chunk]
    new_master, new_momentum = outer_step(scalars, groups, master, momentum, working, cuts, received)
    return new_master[None], new_momentum[None], keys[None]


def solution(mesh):
    return jax.shard_map(
        shards,
        mesh=mesh,
        in_specs=(
            P("replica", "fsdp", None),
            P("replica", "fsdp", None),
            P("replica", "fsdp", None),
            P("replica", "fsdp", None),
            P(),
            P(),
        ),
        out_specs=(
            P("replica", "fsdp", None),
            P("replica", "fsdp", None),
            P("replica", "fsdp", None),
        ),
        check_vma=False,
    )
```

```python
import functools

import jax
import jax.numpy as jnp
from jax import lax
from jax.experimental import pallas as pl
from jax.experimental.pallas import tpu as pltpu
from jax.sharding import PartitionSpec as P

outer_rate = 0.7
momentum_decay = 0.9
PLANE = 4
FIRST = 8
HBM = pl.BlockSpec(memory_space=pltpu.HBM)
SMEM = pl.BlockSpec(memory_space=pltpu.SMEM)
FIRST_LIMIT = pltpu.CompilerParams(vmem_limit_bytes=60 * 2**20)
ARRANGE_LIMIT = pltpu.CompilerParams(vmem_limit_bytes=60 * 2**20)
SMALL = pltpu.CompilerParams(vmem_limit_bytes=16 * 2**20)


def cost(us):
    return pl.CostEstimate(flops=int(us * 1_153_000_000), bytes_accessed=0, transcendentals=0)


COST = dict(add_keys=1, pick=4.5, next_working=4)


def plane_pairs(size, bit):
    return [(i, i ^ bit) for i in range(size)]


def line_pairs(size, to):
    return [(i, to[i // PLANE] * PLANE + i % PLANE) for i in range(size)]


def whole(array):
    return pl.BlockSpec(array.shape, lambda *_: (0,) * array.ndim)


def block_of(line, place, k, distance):
    if line == 4:
        return place ^ ([0, 1, 3, 2][k] * PLANE + distance)
    return ((place % PLANE) ^ distance) + k * PLANE


def arrange_body(width, distances, place, tokens, *refs):
    count = len(distances)
    outs, held, (arrived, left) = refs[:count], refs[count : 2 * count], refs[2 * count :]
    line = outs[0].shape[1] // width
    copies = []
    for i, distance in enumerate(distances):
        for k in range(line):
            start = pl.multiple_of(block_of(line, place[0], k, distance) * width, width)
            copies.append(
                pltpu.make_async_copy(
                    tokens.at[:, pl.ds(start, width)],
                    held[i].at[:, pl.ds(k * width, width)],
                    arrived.at[i * line + k],
                )
            )
    for copy in copies:
        copy.start()
    away = [pltpu.make_async_copy(held[i], outs[i], left.at[i]) for i in range(count)]
    for i in range(count):
        for k in range(line):
            copies[i * line + k].wait()
        away[i].start()
    for copy in away:
        copy.wait()


def arrange_tokens(place, tokens, line, width, distances):
    shape = (tokens.shape[0], line * width)
    return pl.pallas_call(
        functools.partial(arrange_body, width, distances),
        grid=(1,),
        in_specs=[SMEM, HBM],
        out_specs=[HBM] * len(distances),
        out_shape=[jax.ShapeDtypeStruct(shape, tokens.dtype)] * len(distances),
        scratch_shapes=[pltpu.VMEM(shape, tokens.dtype)] * len(distances)
        + [pltpu.SemaphoreType.DMA((line * len(distances),)), pltpu.SemaphoreType.DMA((len(distances),))],
        cost_estimate=cost(0),
        compiler_params=ARRANGE_LIMIT,
        name="arrange_tokens",
    )(place, tokens)


def read_mixing(own_group, partners, mix_weights):
    me = own_group[0]
    numerators = [mix_weights[me, j].astype(jnp.float32) for j in range(5)]
    total = sum(numerators)

    def coefficient(group):
        found = jnp.where(group == me, numerators[0], 0.0)
        for j in range(4):
            found = found + jnp.where(partners[me, j] == group, numerators[j + 1], 0.0)
        return found / total

    return me, coefficient


def others_mixed(groups, me, coefficient, received):
    if groups == 2:
        return coefficient(1 - me) * received[0][...].astype(jnp.float32)
    mixed = jnp.zeros(received[0].shape, jnp.float32)
    for g in range(groups):
        mixed = mixed + jnp.where(g == me, 0.0, coefficient(g)) * received[g][...].astype(jnp.float32)
    return mixed


def first_body(starts, own_group, partners, mix_weights, master, momentum, working, *refs):
    outs, here, arrived = refs[:-4], refs[-4:-1], refs[-1]
    deltas, bases = outs[: len(starts)], outs[len(starts) :]
    copies = [
        pltpu.make_async_copy(there, place, arrived.at[i])
        for i, (there, place) in enumerate(zip((master, working, momentum), here))
    ]
    for copy in copies:
        copy.start()
    me, coefficient = read_mixing(own_group, partners, mix_weights)
    own = coefficient(me)
    copies[0].wait()
    copies[1].wait()
    parts = [slice(start, start + delta.shape[1]) for start, delta in zip(starts, deltas)]
    for part, out in zip(parts, deltas):
        out[...] = (here[0][:, part] - here[1][:, part].astype(jnp.float32)).astype(jnp.bfloat16)
    copies[2].wait()
    for part, out in zip(parts, bases):
        now = here[0][:, part]
        mixed = own * (now - here[1][:, part].astype(jnp.float32))
        new_momentum = momentum_decay * here[2][:, part] + mixed
        out[...] = now - outer_rate * (mixed + momentum_decay * new_momentum)


def first_step(scalars, master, momentum, working, cuts):
    shapes = [(master.shape[0], size) for _, size in cuts]
    outs = pl.pallas_call(
        functools.partial(first_body, [start for start, _ in cuts]),
        grid=(1,),
        in_specs=[SMEM] * 3 + [HBM] * 3,
        out_specs=[pl.BlockSpec(shape, lambda *_: (0, 0)) for shape in shapes] * 2,
        out_shape=[jax.ShapeDtypeStruct(shape, jnp.bfloat16) for shape in shapes]
        + [jax.ShapeDtypeStruct(shape, jnp.float32) for shape in shapes],
        scratch_shapes=[pltpu.VMEM(a.shape, a.dtype) for a in (master, working, momentum)]
        + [pltpu.SemaphoreType.DMA((3,))],
        cost_estimate=cost(0),
        compiler_params=FIRST_LIMIT,
        name="first_step",
    )(*scalars, master, momentum, working)
    return outs[: len(cuts)], outs[len(cuts) :]


def working_body(groups, own_group, partners, mix_weights, base, *refs):
    me, coefficient = read_mixing(own_group, partners, mix_weights)
    mixed = others_mixed(groups, me, coefficient, refs)
    refs[-1][...] = (base[...] - outer_rate * (1 + momentum_decay) * mixed).astype(jnp.bfloat16)


def next_working(scalars, groups, base, received):
    return pl.pallas_call(
        functools.partial(working_body, groups),
        grid=(1,),
        in_specs=[SMEM] * 3 + [whole(a) for a in (base, *received)],
        out_specs=whole(base),
        out_shape=jax.ShapeDtypeStruct(base.shape, jnp.bfloat16),
        cost_estimate=cost(COST["next_working"]),
        compiler_params=SMALL,
        name="next_working",
    )(*scalars, base, *received)


def outer_step_body(groups, starts, own_group, partners, mix_weights, master, momentum, working, *refs):
    received, (new_master, new_momentum) = refs[:-2], refs[-2:]
    each = len(received) // len(starts)
    me, coefficient = read_mixing(own_group, partners, mix_weights)
    own = coefficient(me)
    for i, start in enumerate(starts):
        others = received[i * each : (i + 1) * each]
        part = slice(start, start + others[0].shape[1])
        mixed = own * (master[:, part] - working[:, part].astype(jnp.float32))
        mixed = mixed + others_mixed(groups, me, coefficient, others)
        momentum_now = momentum_decay * momentum[:, part] + mixed
        new_momentum[:, part] = momentum_now
        new_master[:, part] = master[:, part] - outer_rate * (mixed + momentum_decay * momentum_now)


def outer_step(scalars, groups, master, momentum, working, cuts, received):
    shape = jax.ShapeDtypeStruct(master.shape, jnp.float32)
    return pl.pallas_call(
        functools.partial(outer_step_body, groups, [start for start, _ in cuts]),
        grid=(1,),
        in_specs=[SMEM] * 3 + [whole(a) for a in (master, momentum, working, *received)],
        out_specs=[whole(master)] * 2,
        out_shape=[shape, shape],
        cost_estimate=cost(0),
        compiler_params=SMALL,
        name="outer_step",
    )(*scalars, master, momentum, working, *received)


def after(value, *others):
    return lax.optimization_barrier((value, *others))[0]


def product(tokens, pieces, offsets):
    total = None
    for piece, offset in zip(pieces, offsets):
        term = jnp.dot(
            tokens[:, offset : offset + piece.shape[0]], piece[...], preferred_element_type=jnp.float32
        )
        total = term if total is None else total + term
    return total


def early_body(offsets, *refs):
    refs[-1][...] = product(refs[0], refs[1:-1], offsets)


def early_keys(tokens, pieces, offsets):
    span = max(o + p.shape[0] for o, p in zip(offsets, pieces))
    rows, width = tokens.shape[0], pieces[0].shape[1]
    return pl.pallas_call(
        functools.partial(early_body, offsets),
        grid=(1,),
        in_specs=[pl.BlockSpec((rows, span), lambda *_: (0, 0))] + [whole(p) for p in pieces],
        out_specs=pl.BlockSpec((rows, width), lambda *_: (0, 0)),
        out_shape=jax.ShapeDtypeStruct((rows, width), jnp.float32),
        cost_estimate=cost(0),
        compiler_params=SMALL,
        name="early_keys",
    )(tokens, *pieces)


def own_block(line, k, rows, width):
    return pl.BlockSpec((rows, width), lambda i, place: (0, block_of(line, place[0], k, 0)))


def own_early_body(count, each, offsets, place, *refs):
    total = None
    for k in range(count):
        part = slice(k * each, (k + 1) * each)
        term = product(refs[k], refs[count:-1][part], offsets)
        total = term if total is None else total + term
    refs[-1][...] = total


def own_early_keys(place, line, tokens, blocks, width, offsets):
    count, pieces = len(blocks), [piece for block in blocks for piece in block]
    rows, columns = tokens.shape[0], pieces[0].shape[1]
    return pl.pallas_call(
        functools.partial(own_early_body, count, len(offsets), offsets),
        grid_spec=pltpu.PrefetchScalarGridSpec(
            num_scalar_prefetch=1,
            grid=(1,),
            in_specs=[own_block(line, k, rows, width) for k in range(count)] + [whole(p) for p in pieces],
            out_specs=pl.BlockSpec((rows, columns), lambda *_: (0, 0)),
        ),
        out_shape=jax.ShapeDtypeStruct((rows, columns), jnp.float32),
        cost_estimate=cost(0),
        compiler_params=SMALL,
        name="own_early_keys",
    )(place, *([tokens] * count), *pieces)


def last_block(tokens, width):
    rows, span = tokens.shape
    return pl.BlockSpec((rows, width), lambda *_: (0, span // width - 1))


def late_body(offset, place, *refs):
    tokens, sums, piece, outs = refs[:PLANE], refs[PLANE : 2 * PLANE], refs[2 * PLANE], refs[-PLANE:]
    for t, s, o in zip(tokens, sums, outs):
        o[...] = s[...] + product(t, [piece], [offset])


def late_keys(place, line, tokens, sums, width, piece, offset, declared):
    rows, columns = sums[0].shape
    return pl.pallas_call(
        functools.partial(late_body, offset),
        grid_spec=pltpu.PrefetchScalarGridSpec(
            num_scalar_prefetch=1,
            grid=(1,),
            in_specs=[own_block(line, line - 1, rows, width)]
            + [last_block(t, width) for t in tokens[1:]]
            + [whole(a) for a in (*sums, piece)],
            out_specs=[whole(s) for s in sums],
        ),
        out_shape=[jax.ShapeDtypeStruct((rows, columns), jnp.float32)] * PLANE,
        cost_estimate=cost(declared),
        compiler_params=SMALL,
        name="late_keys",
    )(place, *tokens, *sums, piece)


def pick_body(own_first, own, passed, out):
    @pl.when(own_first[0] == 1)
    def _():
        out[...] = own[...]

    @pl.when(own_first[0] == 0)
    def _():
        out[...] = passed[...]


def pick(own_first, own, passed):
    return pl.pallas_call(
        pick_body,
        grid=(1,),
        in_specs=[SMEM, whole(own), whole(passed)],
        out_specs=whole(own),
        out_shape=jax.ShapeDtypeStruct(own.shape, own.dtype),
        cost_estimate=cost(COST["pick"]),
        compiler_params=SMALL,
        name="pick",
    )(own_first, own, passed)


def over_core_body(keep_y, back, to_y):
    to_y[...] = (keep_y[...] + back[...]).astype(to_y.dtype)


def over_core(keep_y, back):
    rows, width = keep_y.shape
    return pl.pallas_call(
        over_core_body,
        grid=(1,),
        in_specs=[whole(keep_y), whole(back)],
        out_specs=whole(keep_y),
        out_shape=jax.ShapeDtypeStruct((rows, width), jnp.bfloat16),
        cost_estimate=cost(0),
        compiler_params=SMALL,
        name="over_core",
    )(keep_y, back)


def over_y_body(*refs):
    keys, start = refs[-1], 0
    for keep, back, there in zip(refs[0:-1:3], refs[1:-1:3], refs[2:-1:3]):
        part = slice(start, start + keep.shape[1])
        keys[:, part] = (keep[...] + back[...] + there[...].astype(jnp.float32)).astype(keys.dtype)
        start = part.stop


def over_y(columns, *terms):
    shape = (terms[0].shape[0], columns)
    return pl.pallas_call(
        over_y_body,
        grid=(1,),
        in_specs=[whole(t) for t in terms],
        out_specs=pl.BlockSpec(shape, lambda *_: (0, 0)),
        out_shape=jax.ShapeDtypeStruct(shape, jnp.bfloat16),
        cost_estimate=cost(0),
        compiler_params=SMALL,
        name="over_y",
    )(*terms)


def shards(master, momentum, working, tokens, partners, mix_weights):
    groups = lax.axis_size("replica")
    size = lax.axis_size("fsdp")
    line = size // PLANE
    place = lax.axis_index("fsdp").astype(jnp.int32)[None]
    scalars = (lax.axis_index("replica").astype(jnp.int32)[None], partners, mix_weights)
    master, momentum, working, tokens = master[0], momentum[0], working[0], tokens[0]
    rows, columns = master.shape
    first = columns * FIRST // 16
    cuts = [(0, first), (first, columns - first)]

    deltas, bases = first_step(scalars, master, momentum, working, cuts)
    def exchange(delta):
        if groups == 2:
            return [lax.ppermute(delta, "replica", [(0, 1), (1, 0)])]
        every = lax.all_gather(delta, "replica", axis=0)
        return [every[g] for g in range(groups)]

    received = [exchange(deltas[0])]

    for_y, for_both, for_core = arrange_tokens(after(place, *deltas), tokens, line, rows, [2, 3, 1])
    from_y = lax.ppermute(for_y, "fsdp", plane_pairs(size, 2))
    from_core = lax.ppermute(for_core, "fsdp", plane_pairs(size, 1))

    received.append([t for t in exchange(deltas[1])])

    fresh = []
    for base, there in zip(bases, received):
        fresh.append(next_working(scalars, groups, base, [after(t, *fresh) for t in there]))
    if line == 4:
        z = place // PLANE
        own_first = jnp.where((z == 1) | (z == 2), 0, 1).astype(jnp.int32)
        far = [lax.ppermute(f, "fsdp", line_pairs(size, [3, 2, 1, 0])) for f in fresh]
        ready = [after(fresh[0], from_core), fresh[1]]
        near = [lax.ppermute(f, "fsdp", line_pairs(size, [1, 0, 3, 2])) for f in ready]
        passed = [far[0], far[1]]
        last = [
            lax.ppermute(pick(own_first, f, g), "fsdp", line_pairs(size, [2, 0, 3, 1]))
            for f, g in zip(fresh, passed)
        ]
        blocks = [fresh, near, far, last]
    else:
        lines = [[k * PLANE + p for k in range(line)] for p in range(PLANE)]
        every = [lax.all_gather(f, "fsdp", axis=0, axis_index_groups=lines) for f in fresh]
        blocks = [[e[k] for e in every] for k in range(line)]
    from_both = lax.ppermute(after(for_both, from_y), "fsdp", plane_pairs(size, 3))
    inputs = [tokens, from_core, from_y, from_both]

    terms = []
    for half, declared in enumerate((COST["add_keys"], 0)):
        early = [[block[half]] for block in blocks[:-1]]
        sums = [own_early_keys(place, line, tokens, early, rows, [0])]
        sums += [early_keys(t, [e for [e] in early], [k * rows for k in range(line - 1)]) for t in inputs[1:]]
        own, for_core, keep_y, for_both = late_keys(
            place, line, inputs, sums, rows, blocks[-1][half], 0, declared
        )
        to_y = over_core(keep_y, lax.ppermute(for_both, "fsdp", plane_pairs(size, 1)))
        back = lax.ppermute(for_core, "fsdp", plane_pairs(size, 1))
        terms += [own, back, lax.ppermute(to_y, "fsdp", plane_pairs(size, 2))]
    keys = over_y(columns, *terms)

    received = [after(r, to_y) for chunk in received for r in chunk]
    new_master, new_momentum = outer_step(scalars, groups, master, momentum, working, cuts, received)
    return new_master[None], new_momentum[None], keys[None]


def solution(mesh):
    return jax.shard_map(
        shards,
        mesh=mesh,
        in_specs=(
            P("replica", "fsdp", None),
            P("replica", "fsdp", None),
            P("replica", "fsdp", None),
            P("replica", "fsdp", None),
            P(),
            P(),
        ),
        out_specs=(
            P("replica", "fsdp", None),
            P("replica", "fsdp", None),
            P("replica", "fsdp", None),
        ),
        check_vma=False,
    )
```
